256 devices in a mesh: row: 32 (over z_hi, y, core), col: 8 (over z_lo, x).
Axes of the slice: x: 4, y: 4, z: 8 (z_hi: 4, z_lo: 2; z = z_hi * 2 + z_lo), core: 2. Of those that a mesh axis runs over, the one named last changes fastest.
Arguments:
- acts: bfloat16 [131072, 4096], P(('row', 'col')), may hold values from -6 to 6
- key_cotangent: bfloat16 [131072, 512], P(('row', 'col')), may hold values from -4 to 4
- error_rows: bfloat16 [32, 8, 512, 4096], P('row', 'col'), may hold values from -12 to 12
- error_cols: float32 [8, 512, 4096], P('col', None, 'row'), may hold values from -2 to 2
Outputs:
- averaged: bfloat16 [512, 4096], P(None, 'row')
- new_error_rows: bfloat16 [32, 8, 512, 4096], P('row', 'col')
- new_error_cols: float32 [8, 512, 4096], P('col', None, 'row')
The draws below stay inside these ranges and needn't reach their ends.
All inputs are finite; a program needn't handle non-finite values. Where the reference program divides by a largest or mean magnitude, that divisor is 1e-20 or more.
Results may differ from the reference program's by a relative error of at most 0.025.
Values may be sent and summed in bfloat16 or wider, within the bound.
No kernel may reach another device: no remote copies, remote signals or barrier semaphores. Data moves between devices by JAX's collectives and lax.ppermute only.
A program may use at most 128 MiB of HBM per device.

```python
import jax
import jax.numpy as jnp
from jax import lax

DW = 4096
KW = 512
TOK_DEV = 512
BLK = 128
TOKENS = 131072
N_ROW = 32
N_COL = 8


def steps_of(key, dims, pieces, smallest, top_value):
    factor_of = 1.0
    for position, shards_of in pieces:
        steps = jax.random.uniform(jax.random.fold_in(jax.random.fold_in(key, 6), position), (shards_of,), jnp.float32, smallest / len(pieces), top_value / len(pieces))
        factor_of = factor_of * jnp.repeat(jnp.exp(steps), dims[position] // shards_of).reshape((-1,) + (1,) * (len(dims) - 1 - position))
    return factor_of


def scatter_about(rng, extent, deviation, most, shards=(), kind=jnp.bfloat16):
    level = steps_of(rng, extent, shards, -0.22, 0.18) if shards else 1.0
    entries = jax.random.normal(rng, extent, jnp.float32) * deviation * level
    return jnp.minimum(jnp.maximum(entries, -most), most).astype(kind)


def setup_inputs(seed: int = 0) -> dict:
    streams_of = jax.random.split(jax.random.key(seed), 5)
    return {
        "acts": scatter_about(streams_of[0], (TOKENS, DW), 1.0, 6.0, ((0, 256),)),
        "key_cotangent": scatter_about(streams_of[1], (TOKENS, KW), 0.5, 4.0, ((0, 256),)),
        "error_rows": scatter_about(streams_of[2], (N_ROW, N_COL, KW, DW), 2.0, 12.0, ((0, 32), (1, 8))),
        "error_cols": scatter_about(streams_of[3], (N_COL, KW, DW), 0.3, 2.0, ((0, 8), (2, 32)), jnp.float32),
    }


def compress(values):
    rows, cols = values.shape
    blocks = values.reshape(rows, cols // BLK, BLK)
    scale = jnp.mean(jnp.abs(blocks), axis=-1, keepdims=True) + 1e-6
    quant = (scale * jnp.tanh(blocks / scale)).reshape(rows, cols).astype(jnp.bfloat16)
    return lax.optimization_barrier(quant).astype(jnp.float32)


def reference(acts, key_cotangent, error_rows, error_cols):
    def one_row(total, row_index):
        def one_device(col_index, residual):
            start = ((row_index * N_COL + col_index) * TOK_DEV).astype(jnp.int32)
            inputs = lax.dynamic_slice_in_dim(acts, start, TOK_DEV, 0)
            grads_out = lax.dynamic_slice_in_dim(key_cotangent, start, TOK_DEV, 0)
            grad = lax.dot_general(grads_out, inputs, (((0,), (0,)), ((), ())), preferred_element_type=jnp.float32)
            carried = grad + residual.astype(jnp.float32)
            sent = compress(carried)
            return (carried - sent).astype(jnp.bfloat16), sent

        residuals = lax.dynamic_index_in_dim(error_rows, row_index, 0, keepdims=False)
        new_res, sent = jax.vmap(one_device)(jnp.arange(N_COL, dtype=jnp.int32), residuals)
        return total + sent, new_res

    start_total = jnp.zeros((N_COL, KW, DW), jnp.float32)
    total, new_error_rows = lax.scan(one_row, start_total, jnp.arange(N_ROW, dtype=jnp.int32))
    row_mean = total / N_ROW
    carried_two = row_mean + error_cols
    sent_two = compress(carried_two.reshape(N_COL * KW, DW)).reshape(N_COL, KW, DW)
    new_error_cols = carried_two - sent_two
    averaged = (jnp.sum(sent_two, axis=0) / N_COL).astype(jnp.bfloat16)
    return averaged, new_error_rows, new_error_cols
```

```python
import functools

import jax
import jax.numpy as jnp
from jax import lax
from jax.experimental import pallas as pl
from jax.experimental.pallas import tpu as pltpu
from jax.sharding import Mesh
from jax.sharding import PartitionSpec as P

BLK = 128
BF = jnp.bfloat16
F32 = jnp.float32
MIB = 2**20
FIRST = ((2, 0), (2, 1), (1, 2), (1, 3), (2, 2), (2, 3), (3, 0), (3, 1))
SECOND = ((1, 0), (1, 1), (3, 2), (3, 3), (0, 0), (0, 1), (0, 2), (0, 3))


def squash(v):
    m = jnp.sum(jnp.abs(v), axis=1, keepdims=True) * (1.0 / BLK) + 1e-6
    return (m * jnp.tanh(v * (1.0 / m))).astype(BF)


def grad_kernel(pos, kc, acts, err, _, newerr, send, keep, kcv, kct, av, ev, sv, kv, gv, ksem, asem, esem, osem, *, table):
    n = len(table)
    zh, y, core = pos[0], pos[1], pos[2]
    kcp = pltpu.make_async_copy(kc, kcv, ksem)
    kcp.start()
    ins, cols = [], []
    for i, (dy, dz) in enumerate(table):
        col = pl.multiple_of((lax.rem(zh + dz, 4) * 4 + lax.rem(y + dy, 4)) * 256, 256)
        cols.append(col)
        a = pltpu.make_async_copy(acts.at[:, pl.ds(col, 256)], av.at[i], asem.at[i])
        e = pltpu.make_async_copy(err.at[:, pl.ds(col, 256)], ev.at[i], esem.at[i])
        a.start()
        e.start()
        ins.append((a, e))
    kcp.wait()
    kct[...] = kcv[...].T

    def product(i):
        for copy in ins[i]:
            copy.wait()
        gv[i % 2] = jnp.dot(kct[...], av[i], preferred_element_type=F32)

    outs = []
    product(0)
    for i in range(n):
        if i + 1 < n:
            product(i + 1)
        g = gv[i % 2]
        q = []
        for k in range(2):
            s = slice(k * BLK, (k + 1) * BLK)
            v = g[:, s] + ev[i, :, s].astype(F32)
            q.append(squash(v))
            ev[i, :, s] = (v - q[k].astype(F32)).astype(BF)
        kv[i] = jnp.where(core == 0, q[0], q[1])
        sv[i] = jnp.where(core == 0, q[1], q[0])
        pairs = (
            (sv.at[i], send.at[i]),
            (kv.at[i], keep.at[i]),
            (ev.at[i], newerr.at[:, pl.ds(cols[i], 256)]),
        )
        for k, (src, dst) in enumerate(pairs):
            copy = pltpu.make_async_copy(src, dst, osem.at[i, k])
            copy.start()
            outs.append(copy)
    for copy in outs:
        copy.wait()


def grad_part(table, pos, kc, acts, err, newerr):
    n = len(table)
    any_space = pl.BlockSpec(memory_space=pl.ANY)
    half = jax.ShapeDtypeStruct((n, 512, BLK), BF)
    body = functools.partial(grad_kernel, table=table)
    operands = (pos, kc, acts, err, newerr)
    aliases = {4: 0}
    if newerr is None:
        operands, aliases = operands[:4], {}
        body = lambda *refs: grad_kernel(*refs[:4], None, *refs[4:], table=table)
    return pl.pallas_call(
        body,
        in_specs=[pl.BlockSpec(memory_space=pltpu.SMEM)] + [any_space] * (len(operands) - 1),
        out_specs=[any_space] * 3,
        out_shape=[jax.ShapeDtypeStruct((512, 4096), BF), half, half],
        scratch_shapes=[
            pltpu.VMEM((512, 512), BF),
            pltpu.VMEM((512, 512), BF),
            pltpu.VMEM((n, 512, 256), BF),
            pltpu.VMEM((n, 512, 256), BF),
            pltpu.VMEM((n, 512, BLK), BF),
            pltpu.VMEM((n, 512, BLK), BF),
            pltpu.VMEM((2, 512, 256), F32),
            pltpu.SemaphoreType.DMA,
            pltpu.SemaphoreType.DMA((n,)),
            pltpu.SemaphoreType.DMA((n,)),
            pltpu.SemaphoreType.DMA((n, 3)),
        ],
        input_output_aliases=aliases,
        compiler_params=pltpu.CompilerParams(vmem_limit_bytes=40 * MIB),
        cost_estimate=pl.CostEstimate(
            flops=2 * 512 * 512 * 256 * n, bytes_accessed=n * MIB, transcendentals=0
        ),
    )(*operands)


def step(x, axis, distance):
    size = lax.axis_size(axis)
    return lax.ppermute(x, axis, [(i, (i + distance) % size) for i in range(size)])


def add(*terms):
    total = terms[0].astype(F32)
    for term in terms[1:]:
        total = total + term.astype(F32)
    return total


def body(acts, key_cotangent, error_rows, error_cols):
    pos = jnp.stack([lax.axis_index("zh"), lax.axis_index("y"), lax.axis_index("core")]).astype(jnp.int32)
    err = error_rows[0, 0]
    newerr, send_1, keep_1 = grad_part(FIRST, pos, key_cotangent, acts, err, None)
    got_1 = step(send_1, "core", 1)
    newerr, send_2, keep_2 = grad_part(SECOND, pos, key_cotangent, acts, err, newerr)
    got_2 = step(send_2, "core", 1)
    up_1 = step(add(keep_1[:4], got_1[:4]).astype(BF), "y", 1)
    down_1 = step(add(keep_1[4:], got_1[4:]).astype(BF), "y", -1)
    up_2 = step(add(keep_2[:2], got_2[:2], up_1[:2]).astype(BF), "y", 1)
    down_2 = step(add(keep_2[2:4], got_2[2:4], down_1[:2]).astype(BF), "y", -1)
    low = add(keep_2[4:6], got_2[4:6], down_1[2:], up_2)
    high = add(keep_2[6:], got_2[6:], up_1[2:], down_2)
    near = step(low[1].astype(BF), "zh", 1)
    far = step(high[0].astype(BF), "zh", 2)
    back = step(high[1].astype(BF), "zh", -1)
    summed = add(low[0], near, far, back)

    carried_two = summed * (1.0 / 32.0) + error_cols[0]
    sent_two = lax.optimization_barrier(squash(carried_two))
    new_cols = (carried_two - sent_two.astype(F32))[None]
    copies = jnp.broadcast_to(sent_two[None], (8, 512, BLK))
    parts = lax.all_to_all(copies, ("zl", "x"), 0, 0, tiled=True)
    averaged = (jnp.sum(parts.astype(F32), axis=0) * 0.125).astype(BF)
    return averaged, newerr[None, None], new_cols


def solution(mesh):
    fine = Mesh(mesh.devices.reshape(4, 4, 2, 2, 4), ("zh", "y", "core", "zl", "x"))
    row, col = ("zh", "y", "core"), ("zl", "x")
    in_specs = (
        P(row + col, None),
        P(row + col, None),
        P(row, col, None, None),
        P(col, None, row),
    )
    out_specs = (P(None, row), P(row, col, None, None), P(col, None, row))
    return jax.shard_map(body, mesh=fine, in_specs=in_specs, out_specs=out_specs, check_vma=False)
```

```python
import functools

import jax
import jax.numpy as jnp
from jax import lax
from jax.experimental import pallas as pl
from jax.experimental.pallas import tpu as pltpu
from jax.sharding import Mesh
from jax.sharding import PartitionSpec as P

BLK = 128
BF = jnp.bfloat16
F32 = jnp.float32
MIB = 2**20
CHUNKS = ((0, 512),)


def partner(which, i, core):
    flip = lax.bitwise_xor(i, 1)
    turn = 3 - i
    return jnp.where(core == which, flip, turn)


def ring_pairs(which, shape, ring, core):
    def linear(pos):
        out = 0
        for p, n in zip(pos, shape):
            out = out * n + p
        return out

    pairs = []
    for r in range(4):
        for c in range(2):
            src, dst = [0, 0], [0, 0]
            src[ring], src[core] = r, c
            dst[ring], dst[core] = (r ^ 1 if c == which else 3 - r), c
            pairs.append((linear(src), linear(dst)))
    return pairs


def squash(v):
    m = jnp.sum(jnp.abs(v), axis=1, keepdims=True) * (1.0 / BLK) + 1e-6
    return (m * jnp.tanh(v * (1.0 / m))).astype(BF)


def grad_kernel(pos, kc, acts, err, newerr, send, keep, kcv, kct, av, ev, sv, kv, gv, ksem, asem, osem, *, rows):
    n = 8
    row0, count = rows
    kcp = pltpu.make_async_copy(kc.at[:, pl.ds(row0, count)], kcv, ksem)
    kcp.start()
    ins, cols = [], []
    for i in range(n):
        ins.append([])
        cols.append([])
        for side in range(2):
            col = pl.multiple_of(pos[side * n + i] * BLK, BLK)
            cols[i].append(col)
            half = pl.ds(side * BLK, BLK)
            a = pltpu.make_async_copy(acts.at[:, pl.ds(col, BLK)], av.at[i, :, half], asem.at[i, side, 0])
            e = pltpu.make_async_copy(
                err.at[pl.ds(row0, count), pl.ds(col, BLK)], ev.at[i, :, half], asem.at[i, side, 1]
            )
            a.start()
            e.start()
            ins[i] += [a, e]
    kcp.wait()
    kct[...] = kcv[...].T

    def product(i):
        for copy in ins[i]:
            copy.wait()
        gv[i % 2] = jnp.dot(kct[...], av[i], preferred_element_type=F32)

    outs = []
    product(0)
    for i in range(n):
        if i + 1 < n:
            product(i + 1)
        g = gv[i % 2]
        for k, out in enumerate((kv, sv)):
            s = slice(k * BLK, (k + 1) * BLK)
            v = g[:, s] + ev[i, :, s].astype(F32)
            q = squash(v)
            out[i] = q
            ev[i, :, s] = (v - q.astype(F32)).astype(BF)
        pairs = [(sv.at[i], send.at[i]), (kv.at[i], keep.at[i])]
        for side in range(2):
            half = pl.ds(side * BLK, BLK)
            pairs.append((ev.at[i, :, half], newerr.at[pl.ds(row0, count), pl.ds(cols[i][side], BLK)]))
        for k, (src, dst) in enumerate(pairs):
            copy = pltpu.make_async_copy(src, dst, osem.at[i, k])
            copy.start()
            outs.append(copy)
    for copy in outs:
        copy.wait()


def grad_part(pos, kc, acts, err, newerr, rows, limit):
    n = 8
    count = rows[1]
    in_hbm = pl.BlockSpec(memory_space=pltpu.HBM)
    free = pl.BlockSpec(memory_space=pl.ANY)
    half = jax.ShapeDtypeStruct((n, count, BLK), BF)
    operands, aliases = (pos, kc, acts, err), {}
    body = functools.partial(grad_kernel, rows=rows)
    if newerr is not None:
        operands, aliases = operands + (newerr,), {4: 0}
        body = lambda *refs: grad_kernel(*refs[:4], *refs[5:], rows=rows)
    return pl.pallas_call(
        body,
        in_specs=[pl.BlockSpec(memory_space=pltpu.SMEM)] + [in_hbm] * (len(operands) - 1),
        out_specs=[in_hbm, free, free],
        out_shape=[jax.ShapeDtypeStruct((512, 4096), BF), half, half],
        scratch_shapes=[
            pltpu.VMEM((512, count), BF),
            pltpu.VMEM((count, 512), BF),
            pltpu.VMEM((n, 512, 256), BF),
            pltpu.VMEM((n, count, 256), BF),
            pltpu.VMEM((n, count, BLK), BF),
            pltpu.VMEM((n, count, BLK), BF),
            pltpu.VMEM((2, count, 256), F32),
            pltpu.SemaphoreType.DMA,
            pltpu.SemaphoreType.DMA((n, 2, 2)),
            pltpu.SemaphoreType.DMA((n, 4)),
        ],
        input_output_aliases=aliases,
        compiler_params=pltpu.CompilerParams(vmem_limit_bytes=limit * MIB),
        cost_estimate=pl.CostEstimate(
            flops=2 * count * 512 * 256 * n, bytes_accessed=n * MIB, transcendentals=0
        ),
    )(*operands)


def add(*terms):
    total = terms[0].astype(F32)
    for term in terms[1:]:
        total = total + term.astype(F32)
    return total


def columns():
    zh, y, core = (lax.axis_index(a) for a in ("zh", "y", "core"))

    def blocks(which_y, c):
        z1, z2 = partner(0, zh, c), partner(1, zh, c)
        zs = (zh, z2, z1, lax.bitwise_xor(zh, 2))
        y1, y2 = partner(0, y, c), partner(1, y, c)
        ys = (y1, lax.bitwise_xor(y, 2)) if which_y == 0 else (y, y2)
        return [(z * 4 + t) * 2 + c for t in ys for z in zs]

    return [
        jnp.stack(blocks(part, core) + blocks(part, 1 - core)).astype(jnp.int32) for part in range(2)
    ]


def y_step(x, which):
    return lax.ppermute(x, ("y", "core"), ring_pairs(which, (4, 2), 0, 1))


def z_step(x, which):
    pairs = []
    for s, d in ring_pairs(which, (4, 2), 0, 1):
        for y in range(4):
            pairs.append(((s // 2 * 4 + y) * 2 + s % 2, (d // 2 * 4 + y) * 2 + d % 2))
    return lax.ppermute(x, ("zh", "y", "core"), pairs)


def x_step(x, which):
    pairs = []
    for s, d in ring_pairs(which, (2, 4), 1, 0):
        for zl in range(2):
            pairs.append(((s // 4 * 2 + zl) * 4 + s % 4, (d // 4 * 2 + zl) * 4 + d % 4))
    return lax.ppermute(x, ("core", "zl", "x"), pairs)


def swap(x, axis):
    return lax.ppermute(x, axis, [(0, 1), (1, 0)])


def body(acts, key_cotangent, error_rows, error_cols):
    first, second = columns()
    err = error_rows[0, 0]
    newerr = None
    averaged, new_cols = [], []
    for rows in CHUNKS:
        newerr, send, keep = grad_part(first, key_cotangent, acts, err, newerr, rows, 60)
        ahead = add(keep, swap(send, "core")).astype(BF)
        second, ahead = lax.optimization_barrier((second, ahead))
        got_1 = y_step(ahead, 0)
        newerr, send, keep = grad_part(second, key_cotangent, acts, err, newerr, rows, 57)
        swapped = swap(send, "core")
        mine = add(keep, swapped, got_1)
        got_2 = y_step(mine[4:].astype(BF), 1)
        mine = add(mine[:4], got_2)
        got_3 = z_step(mine[2:].astype(BF), 0)
        mine = add(mine[:2], got_3)
        got_4 = z_step(mine[1].astype(BF), 1)
        summed = add(mine[0], got_4)

        carried_two = summed * (1.0 / 32.0) + error_cols[0, rows[0] : rows[0] + rows[1]]
        sent_two = lax.optimization_barrier(squash(carried_two))
        new_cols.append(carried_two - sent_two.astype(F32))
        total = add(sent_two, swap(sent_two, "zl"))
        for which in range(2):
            total = add(total, x_step(total.astype(BF), which))
        averaged.append((total * 0.125).astype(BF))
    return jnp.concatenate(averaged), newerr[None, None], jnp.concatenate(new_cols)[None]


def solution(mesh):
    fine = Mesh(mesh.devices.reshape(4, 4, 2, 2, 4), ("zh", "y", "core", "zl", "x"))
    row, col = ("zh", "y", "core"), ("zl", "x")
    in_specs = (
        P(row + col, None),
        P(row + col, None),
        P(row, col, None, None),
        P(col, None, row),
    )
    out_specs = (P(None, row), P(row, col, None, None), P(col, None, row))
    return jax.shard_map(body, mesh=fine, in_specs=in_specs, out_specs=out_specs, check_vma=False)
```

```python
import functools

import jax
import jax.numpy as jnp
from jax import lax
from jax.experimental import pallas as pl
from jax.experimental.pallas import tpu as pltpu
from jax.sharding import Mesh
from jax.sharding import PartitionSpec as P

BLK = 128
BF = jnp.bfloat16
F32 = jnp.float32
MIB = 2**20
CHUNKS = 2
DEPTH = 4


def partner(which, i, core):
    flip = lax.bitwise_xor(i, 1)
    turn = 3 - i
    return jnp.where(core == which, flip, turn)


def ring_pairs(which, shape, ring, core):
    def linear(pos):
        out = 0
        for p, n in zip(pos, shape):
            out = out * n + p
        return out

    pairs = []
    for r in range(4):
        for c in range(2):
            src, dst = [0, 0], [0, 0]
            src[ring], src[core] = r, c
            dst[ring], dst[core] = (r ^ 1 if c == which else 3 - r), c
            pairs.append((linear(src), linear(dst)))
    return pairs


def squash(v):
    m = jnp.sum(jnp.abs(v), axis=1, keepdims=True) * (1.0 / BLK) + 1e-6
    return (m * jnp.tanh(v * (1.0 / m))).astype(BF)


def grad_kernel(pos, kc, acts, err, newerr, send, keep, kcv, kct, av, ev, gv, ksem, asem, osem, *, part):
    n = 8
    zh, y, core = pos[0], pos[1], pos[2]
    other = 1 - core
    zs = (zh, partner(1, zh, core), partner(0, zh, core), lax.bitwise_xor(zh, 2))
    swapped = (0, 2, 1, 3)
    y1, y2 = partner(0, y, core), partner(1, y, core)
    if part == 0:
        whole, split, base = lax.bitwise_xor(y, 2), (y1, y2), (4, 0)
    else:
        whole, split, base = y, (y2, y1), (0, 4)
    items = [([(z * 4 + whole) * 256], base[0] + k, base[0] + swapped[k]) for k, z in enumerate(zs)]
    for k, z in enumerate(zs):
        left = ((z * 4 + split[0]) * 2 + core) * BLK
        right = ((z * 4 + split[1]) * 2 + other) * BLK
        items.append(([left, right], base[1] + k, base[1] + swapped[k]))

    def windows(i):
        starts = items[i][0]
        width = 256 // len(starts)
        for k, start in enumerate(starts):
            yield k, pl.ds(pl.multiple_of(start, width), width), pl.ds(k * width, width)

    def loads(i):
        for k, col, half in windows(i):
            yield pltpu.make_async_copy(acts.at[:, col], av.at[i, :, half], asem.at[i, k, 0])
            yield pltpu.make_async_copy(err.at[:, col], ev.at[i, :, half], asem.at[i, k, 1])

    def stores(i):
        for k, col, half in windows(i):
            yield pltpu.make_async_copy(ev.at[i, :, half], newerr.at[:, col], osem.at[i, k])

    def product(i):
        for copy in loads(i):
            copy.wait()
        gv[i % 2] = jnp.dot(kct[...], av[i], preferred_element_type=F32)

    load_kc = pltpu.make_async_copy(kc, kcv, ksem)
    load_kc.start()
    for i in range(DEPTH):
        for copy in loads(i):
            copy.start()
    load_kc.wait()
    kct[...] = kcv[...].T
    product(0)
    for i in range(n):
        if i + DEPTH < n:
            for copy in loads(i + DEPTH):
                copy.start()
        if i + 1 < n:
            product(i + 1)
        q = []
        for k in range(2):
            s = slice(k * BLK, (k + 1) * BLK)
            v = gv[i % 2, :, s] + ev[i, :, s].astype(F32)
            q.append(squash(v))
            ev[i, :, s] = (v - q[k].astype(F32)).astype(BF)
        starts, kept, sent = items[i]
        if len(starts) == 1:
            q = [jnp.where(core == 0, q[0], q[1]), jnp.where(core == 0, q[1], q[0])]
        keep[kept] = q[0]
        send[sent] = q[1]
        for copy in stores(i):
            copy.start()
    for i in range(n):
        for copy in stores(i):
            copy.wait()


def grad_part(pos, kc, acts, err, newerr, part):
    n = 8
    free = pl.BlockSpec(memory_space=pl.ANY)
    near = pl.BlockSpec(memory_space=pltpu.VMEM)
    operands, aliases = (kc, acts, err), {}
    body = functools.partial(grad_kernel, part=part)
    if newerr is not None:
        operands, aliases = operands + (newerr,), {4: 0}
        body = lambda *refs: grad_kernel(*refs[:4], *refs[5:], part=part)
    operands = [pltpu.with_memory_space_constraint(o, pltpu.HBM) for o in operands]
    half = pltpu.VMEM((n, 512, BLK), BF)
    return pl.pallas_call(
        body,
        in_specs=[pl.BlockSpec(memory_space=pltpu.SMEM)] + [free] * len(operands),
        out_specs=[free, near, near],
        out_shape=[pltpu.HBM((512, 4096), BF), half, half],
        scratch_shapes=[
            pltpu.VMEM((512, 512), BF),
            pltpu.VMEM((512, 512), BF),
            pltpu.VMEM((n, 512, 256), BF),
            pltpu.VMEM((n, 512, 256), BF),
            pltpu.VMEM((2, 512, 256), F32),
            pltpu.SemaphoreType.DMA,
            pltpu.SemaphoreType.DMA((n, 2, 2)),
            pltpu.SemaphoreType.DMA((n, 2)),
        ],
        input_output_aliases=aliases,
        compiler_params=pltpu.CompilerParams(vmem_limit_bytes=24 * MIB),
        cost_estimate=pl.CostEstimate(
            flops=2 * 512 * 512 * 256 * n, bytes_accessed=n * MIB, transcendentals=0
        ),
    )(pos, *operands)


def add(*terms):
    total = terms[0].astype(F32)
    for term in terms[1:]:
        total = total + term.astype(F32)
    return total


def y_step(x, which):
    return lax.ppermute(x, ("y", "core"), ring_pairs(which, (4, 2), 0, 1))


def z_step(x, which):
    pairs = []
    for s, d in ring_pairs(which, (4, 2), 0, 1):
        for y in range(4):
            pairs.append(((s // 2 * 4 + y) * 2 + s % 2, (d // 2 * 4 + y) * 2 + d % 2))
    return lax.ppermute(x, ("zh", "y", "core"), pairs)


def swap(x, axis):
    return lax.ppermute(x, axis, [(0, 1), (1, 0)])


def body(acts, key_cotangent, error_rows, error_cols):
    pos = jnp.stack([lax.axis_index(a) for a in ("zh", "y", "core")]).astype(jnp.int32)
    err = error_rows[0, 0]
    parts = [slice(r, r + 512 // CHUNKS) for r in range(0, 512, 512 // CHUNKS)]
    newerr, send, keep = grad_part(pos, key_cotangent, acts, err, None, 0)
    swapped = swap(send, "core")
    ahead = add(keep, swapped).astype(BF)
    pos, ahead = lax.optimization_barrier((pos, ahead))
    got = y_step(ahead, 0)
    newerr, send, keep = grad_part(pos, key_cotangent, acts, err, newerr, 1)
    swapped = swap(send, "core")
    mine = [add(keep[:, p], swapped[:, p], got[:, p]) for p in parts]
    got = [y_step(m[4:].astype(BF), 1) for m in mine]
    mine = [add(m[:4], g) for m, g in zip(mine, got)]
    got = [z_step(m[2:].astype(BF), 0) for m in mine]
    mine = [add(m[:2], g) for m, g in zip(mine, got)]
    got = [z_step(m[1].astype(BF), 1) for m in mine]
    summed = jnp.concatenate([add(m[0], g) for m, g in zip(mine, got)])

    carried_two = summed * (1.0 / 32.0) + error_cols[0]
    sent_two = lax.optimization_barrier(squash(carried_two))
    new_cols = carried_two - sent_two.astype(F32)
    total = add(sent_two, swap(sent_two, "zl"))
    near = [
        lax.ppermute(total.astype(BF), "x", [(i, (i + d) % 4) for i in range(4)]) for d in (1, 3, 2)
    ]
    averaged = (add(total, *near) * 0.125).astype(BF)
    return averaged, newerr[None, None], new_cols[None]


def solution(mesh):
    fine = Mesh(mesh.devices.reshape(4, 4, 2, 2, 4), ("zh", "y", "core", "zl", "x"))
    row, col = ("zh", "y", "core"), ("zl", "x")
    in_specs = (
        P(row + col, None),
        P(row + col, None),
        P(row, col, None, None),
        P(col, None, row),
    )
    out_specs = (P(None, row), P(row, col, None, None), P(col, None, row))
    return jax.shard_map(body, mesh=fine, in_specs=in_specs, out_specs=out_specs, check_vma=False)
```

```python
import functools

import jax
import jax.numpy as jnp
from jax import lax
from jax.experimental import pallas as pl
from jax.experimental.pallas import tpu as pltpu
from jax.sharding import Mesh
from jax.sharding import PartitionSpec as P

BLK = 128
BF = jnp.bfloat16
F32 = jnp.float32
MIB = 2**20
CHUNKS = 2
DEPTH = 4
PARTS = (
    tuple(("far", i) for i in range(4)),
    tuple(("one", i) for i in range(4)) + tuple(("two", i) for i in range(4)),
    tuple(("own", i) for i in range(4)),
)
SEND_SLOT = ((0, 2, 1, 3), (0, 2, 1, 3, 4, 6, 5, 7), (0, 2, 1, 3))


def partner(which, i, core):
    flip = lax.bitwise_xor(i, 1)
    turn = 3 - i
    return jnp.where(core == which, flip, turn)


def ring_pairs(which, shape, ring, core):
    def linear(pos):
        out = 0
        for p, n in zip(pos, shape):
            out = out * n + p
        return out

    pairs = []
    for r in range(4):
        for c in range(2):
            src, dst = [0, 0], [0, 0]
            src[ring], src[core] = r, c
            dst[ring], dst[core] = (r ^ 1 if c == which else 3 - r), c
            pairs.append((linear(src), linear(dst)))
    return pairs


def squash(v):
    m = jnp.sum(jnp.abs(v), axis=1, keepdims=True) * (1.0 / BLK) + 1e-6
    return (m * jnp.tanh(v * (1.0 / m))).astype(BF)


def items_of(pos, kind):
    zh, y, core = pos[0], pos[1], pos[2]
    other = 1 - core
    zs = (zh, partner(1, zh, core), partner(0, zh, core), lax.bitwise_xor(zh, 2))
    y1, y2 = partner(0, y, core), partner(1, y, core)
    if kind in ("far", "own"):
        whole = y if kind == "own" else lax.bitwise_xor(y, 2)
        return [[(z * 4 + whole) * 256] for z in zs]
    left, right = (y1, y2) if kind == "one" else (y2, y1)
    return [[((z * 4 + left) * 2 + core) * BLK, ((z * 4 + right) * 2 + other) * BLK] for z in zs]


def windows(starts):
    width = 256 // len(starts)
    for k, start in enumerate(starts):
        yield k, pl.ds(pl.multiple_of(start, width), width), pl.ds(k * width, width)


def grad_kernel(pos, kc, acts, err, *refs, part):
    if part == 0:
        send, keep, ev, kct, kcv, av, gv, asem, ksem = refs
    else:
        send, keep, ev, av, gv, asem = refs
        kct = kc
    core = pos[2]
    kinds = {kind: items_of(pos, kind) for kind, _ in PARTS[part]}
    items = [kinds[kind][i] for kind, i in PARTS[part]]
    n = len(items)

    def loads(i):
        for k, col, half in windows(items[i]):
            yield pltpu.make_async_copy(acts.at[:, col], av.at[i, :, half], asem.at[i, k, 0])
            yield pltpu.make_async_copy(err.at[:, col], ev.at[i, :, half], asem.at[i, k, 1])

    if part == 0:
        load_kc = pltpu.make_async_copy(kc, kcv, ksem)
        load_kc.start()
    for i in range(DEPTH):
        for copy in loads(i):
            copy.start()
    if part == 0:
        load_kc.wait()
        kct[...] = kcv[...].T
    for copy in loads(0):
        copy.wait()
    gv[0] = jnp.dot(kct[...], av[0], preferred_element_type=F32)
    for i in range(n):
        if i + DEPTH < n:
            for copy in loads(i + DEPTH):
                copy.start()
        if i + 1 < n:
            for copy in loads(i + 1):
                copy.wait()
        for r in range(0, 512, 256):
            rows = slice(r, r + 256)
            if i + 1 < n:
                gv[(i + 1) % 2, rows] = jnp.dot(kct[rows], av[i + 1], preferred_element_type=F32)
            q = []
            for k in range(2):
                s = slice(k * BLK, (k + 1) * BLK)
                v = gv[i % 2, rows, s] + ev[i, rows, s].astype(F32)
                q.append(squash(v))
                ev[i, rows, s] = (v - q[k].astype(F32)).astype(BF)
            if len(items[i]) == 1:
                q = [jnp.where(core == 0, q[0], q[1]), jnp.where(core == 0, q[1], q[0])]
            keep[i, rows] = q[0]
            send[SEND_SLOT[part][i], rows] = q[1]


def grad_part(pos, kc, acts, err, part):
    n = len(PARTS[part])
    in_hbm = pl.BlockSpec(memory_space=pl.ANY)
    near = pl.BlockSpec(memory_space=pltpu.VMEM)
    in_smem = pl.BlockSpec(memory_space=pltpu.SMEM)
    pin = lambda o: pltpu.with_memory_space_constraint(o, pltpu.HBM)
    half = pltpu.VMEM((n, 512, BLK), BF)
    outs = [half, half, pltpu.VMEM((n, 512, 256), BF)]
    scratch = [
        pltpu.VMEM((n, 512, 256), BF),
        pltpu.VMEM((2, 512, 256), F32),
        pltpu.SemaphoreType.DMA((n, 2, 2)),
    ]
    if part == 0:
        outs.append(pltpu.VMEM((512, 512), BF))
        scratch = [pltpu.VMEM((512, 512), BF), *scratch, pltpu.SemaphoreType.DMA]
    return pl.pallas_call(
        functools.partial(grad_kernel, part=part),
        in_specs=[in_smem, in_hbm if part == 0 else near, in_hbm, in_hbm],
        out_specs=[near] * len(outs),
        out_shape=outs,
        scratch_shapes=scratch,
        compiler_params=pltpu.CompilerParams(vmem_limit_bytes=24 * MIB),
        cost_estimate=pl.CostEstimate(
            flops=10**6, bytes_accessed=10**4, transcendentals=0
        ),
    )(pos, pin(kc) if part == 0 else kc, pin(acts), pin(err))


def store_kernel(pos, *refs):
    blocks, (newerr, sem) = refs[: len(PARTS)], refs[len(PARTS) :]
    copies = []
    for part, members in enumerate(PARTS):
        for i, (kind, item) in enumerate(members):
            for k, col, half in windows(items_of(pos, kind)[item]):
                copies.append(
                    pltpu.make_async_copy(
                        blocks[part].at[i, :, half], newerr.at[:, col], sem.at[part, i, k]
                    )
                )
    for copy in copies:
        copy.start()
    for copy in copies:
        copy.wait()


def store_residual(pos, blocks):
    near = pl.BlockSpec(memory_space=pltpu.VMEM)
    return pl.pallas_call(
        store_kernel,
        in_specs=[pl.BlockSpec(memory_space=pltpu.SMEM)] + [near] * len(PARTS),
        out_specs=pl.BlockSpec(memory_space=pl.ANY),
        out_shape=pltpu.HBM((512, 4096), BF),
        scratch_shapes=[pltpu.SemaphoreType.DMA((len(PARTS), max(map(len, PARTS)), 2))],
        compiler_params=pltpu.CompilerParams(vmem_limit_bytes=24 * MIB),
        cost_estimate=pl.CostEstimate(flops=0, bytes_accessed=8 * MIB, transcendentals=0),
    )(pos, *blocks)


def add(*terms):
    total = terms[0].astype(F32)
    for term in terms[1:]:
        total = total + term.astype(F32)
    return total


def y_step(x, which):
    return lax.ppermute(x, ("y", "core"), ring_pairs(which, (4, 2), 0, 1))


def z_step(x, which):
    pairs = []
    for s, d in ring_pairs(which, (4, 2), 0, 1):
        for y in range(4):
            pairs.append(((s // 2 * 4 + y) * 2 + s % 2, (d // 2 * 4 + y) * 2 + d % 2))
    return lax.ppermute(x, ("zh", "y", "core"), pairs)


def swap(x, axis):
    return lax.ppermute(x, axis, [(0, 1), (1, 0)])


def body(acts, key_cotangent, error_rows, error_cols):
    pos = jnp.stack([lax.axis_index(a) for a in ("zh", "y", "core")]).astype(jnp.int32)
    err = error_rows[0, 0]
    parts = [slice(r, r + 512 // CHUNKS) for r in range(0, 512, 512 // CHUNKS)]
    tie = lax.optimization_barrier
    send, keep, err_0, kct = grad_part(pos, key_cotangent, acts, err, 0)
    ahead = add(keep, swap(send, "core")).astype(BF)
    pos, ahead = tie((pos, ahead))
    got_0 = y_step(ahead, 0)
    send, keep, err_1 = grad_part(pos, kct, acts, err, 1)
    near = [swap(send[k : k + 2], "core") for k in range(0, 8, 2)]
    one, two = jnp.concatenate(near[: 2]), near[2 :]
    ahead = add(keep[:4], one).astype(BF)
    ahead, two = tie((ahead, two))
    got_1 = y_step(ahead, 0)
    ahead = add(keep[4:], jnp.concatenate(two), got_0).astype(BF)
    pos, ahead = tie((pos, ahead))
    got_2 = y_step(ahead, 1)
    send, keep, err_2 = grad_part(pos, kct, acts, err, 2)
    got = tie(add(got_1, got_2))
    swapped = swap(send, "core")
    mine = [add(keep[:, p], swapped[:, p], got[:, p]) for p in parts]
    pos, *mine = tie((pos, *mine))
    newerr = store_residual(pos, (err_0, err_1, err_2))
    got = [z_step(m[2:].astype(BF), 0) for m in mine]
    mine = [add(m[:2], g) for m, g in zip(mine, got)]
    got = [z_step(m[1].astype(BF), 1) for m in mine]
    summed = jnp.concatenate([add(m[0], g) for m, g in zip(mine, got)])

    carried_two = summed * (1.0 / 32.0) + error_cols[0]
    sent_two = lax.optimization_barrier(squash(carried_two))
    new_cols = carried_two - sent_two.astype(F32)
    total = add(sent_two, swap(sent_two, "zl"))
    near = [
        lax.ppermute(total.astype(BF), "x", [(i, (i + d) % 4) for i in range(4)]) for d in (1, 3, 2)
    ]
    averaged = (add(total, *near) * 0.125).astype(BF)
    return averaged, newerr[None, None], new_cols[None]


def solution(mesh):
    fine = Mesh(mesh.devices.reshape(4, 4, 2, 2, 4), ("zh", "y", "core", "zl", "x"))
    row, col = ("zh", "y", "core"), ("zl", "x")
    in_specs = (
        P(row + col, None),
        P(row + col, None),
        P(row, col, None, None),
        P(col, None, row),
    )
    out_specs = (P(None, row), P(row, col, None, None), P(col, None, row))
    return jax.shard_map(body, mesh=fine, in_specs=in_specs, out_specs=out_specs, check_vma=False)
```

```python
import functools

import jax
import jax.numpy as jnp
from jax import lax
from jax.experimental import pallas as pl
from jax.experimental.pallas import tpu as pltpu
from jax.sharding import Mesh
from jax.sharding import PartitionSpec as P

BLK = 128
BF = jnp.bfloat16
F32 = jnp.float32
MIB = 2**20
CHUNKS = 2
DEPTH = 4
GROUP = (2, 1, 1)
READY = 4
PARTS = (
    tuple(("far", i) for i in range(4)),
    tuple(("one", i) for i in range(4)) + tuple(("two", i) for i in range(4)),
    tuple(("own", i) for i in range(4)),
)
SEND_SLOT = ((0, 2, 1, 3), (0, 2, 1, 3, 4, 6, 5, 7), (0, 2, 1, 3))


def partner(which, i, core):
    flip = lax.bitwise_xor(i, 1)
    turn = 3 - i
    return jnp.where(core == which, flip, turn)


def ring_pairs(which, shape, ring, core):
    def linear(pos):
        out = 0
        for p, n in zip(pos, shape):
            out = out * n + p
        return out

    pairs = []
    for r in range(4):
        for c in range(2):
            src, dst = [0, 0], [0, 0]
            src[ring], src[core] = r, c
            dst[ring], dst[core] = (r ^ 1 if c == which else 3 - r), c
            pairs.append((linear(src), linear(dst)))
    return pairs


def squash(v):
    m = jnp.sum(jnp.abs(v), axis=1, keepdims=True) * (1.0 / BLK) + 1e-6
    return (m * jnp.tanh(v * (1.0 / m))).astype(BF)


def items_of(pos, kind):
    zh, y, core = pos[0], pos[1], pos[2]
    other = 1 - core
    zs = (zh, partner(1, zh, core), partner(0, zh, core), lax.bitwise_xor(zh, 2))
    y1, y2 = partner(0, y, core), partner(1, y, core)
    if kind in ("far", "own"):
        whole = y if kind == "own" else lax.bitwise_xor(y, 2)
        return [[(z * 4 + whole) * 256] for z in zs]
    left, right = (y1, y2) if kind == "one" else (y2, y1)
    return [[((z * 4 + left) * 2 + core) * BLK, ((z * 4 + right) * 2 + other) * BLK] for z in zs]


def columns_of(pos, part):
    kinds = {kind: items_of(pos, kind) for kind, _ in PARTS[part]}
    return [kinds[kind][i] for kind, i in PARTS[part]]


def windows(starts, offset=0):
    width = 256 // len(starts)
    for k, start in enumerate(starts):
        yield k, pl.ds(pl.multiple_of(start, width), width), pl.ds(offset + k * width, width)


def grad_kernel(pos, kc, acts, err, *refs, part):
    if part == 0:
        send, keep, ev, kct, ready_a, ready_e, kcv, av, gv, asem, rsem, ksem = refs
    elif part == 1:
        ready_a, ready_e, send, keep, ev, av, gv, asem = refs
        kct = kc
    else:
        send, keep, ev, av, gv, asem = refs
        kct = kc
    core = pos[2]
    items = columns_of(pos, part)
    n, group = len(items), GROUP[part]
    first = READY if part == 1 else 0

    def loads(i):
        for k, col, half in windows(items[i], 256 * (i % group)):
            yield pltpu.make_async_copy(acts.at[:, col], av.at[i // group, :, half], asem.at[i, k, 0])
        for k, col, half in windows(items[i]):
            yield pltpu.make_async_copy(err.at[:, col], ev.at[i, :, half], asem.at[i, k, 1])

    def loads_ahead():
        for i, item in enumerate(columns_of(pos, 1)[:READY]):
            for k, col, half in windows(item):
                yield pltpu.make_async_copy(acts.at[:, col], ready_a.at[i, :, half], rsem.at[i, k, 0])
                yield pltpu.make_async_copy(err.at[:, col], ready_e.at[i, :, half], rsem.at[i, k, 1])

    def ready(p):
        for i in range(p * group, (p + 1) * group):
            if i >= first:
                for copy in loads(i):
                    copy.wait()

    def source(p):
        return ready_a[p] if p < first else av[p]

    if part == 0:
        load_kc = pltpu.make_async_copy(kc, kcv, ksem)
        load_kc.start()
    for i in range(first, first + DEPTH):
        for copy in loads(i):
            copy.start()
    if part == 0:
        load_kc.wait()
        kct[...] = kcv[...].T
    ready(0)
    if part == 0:
        for copy in loads_ahead():
            copy.start()
    gv[0] = jnp.dot(kct[...], source(0), preferred_element_type=F32)
    for p in range(n // group):
        members = range(p * group, (p + 1) * group)
        for i in members:
            if i >= first and i + DEPTH < n:
                for copy in loads(i + DEPTH):
                    copy.start()
        more = p + 1 < n // group
        if more:
            ready(p + 1)
        for r in range(0, 512, 256):
            rows = slice(r, r + 256)
            if more:
                gv[(p + 1) % 2, rows] = jnp.dot(kct[rows], source(p + 1), preferred_element_type=F32)
            for i in members:
                q = []
                for k in range(2):
                    s = slice(k * BLK, (k + 1) * BLK)
                    t = 256 * (i % group) + k * BLK
                    residual = (ready_e if i < first else ev)[i, rows, s]
                    v = gv[p % 2, rows, t : t + BLK] + residual.astype(F32)
                    q.append(squash(v))
                    ev[i, rows, s] = (v - q[k].astype(F32)).astype(BF)
                if len(items[i]) == 1:
                    q = [jnp.where(core == 0, q[0], q[1]), jnp.where(core == 0, q[1], q[0])]
                keep[i, rows] = q[0]
                send[SEND_SLOT[part][i], rows] = q[1]
    if part == 0:
        for copy in loads_ahead():
            copy.wait()


def grad_part(pos, kc, acts, err, part, ahead=()):
    n, group = len(PARTS[part]), GROUP[part]
    in_hbm = pl.BlockSpec(memory_space=pl.ANY)
    near = pl.BlockSpec(memory_space=pltpu.VMEM)
    in_smem = pl.BlockSpec(memory_space=pltpu.SMEM)
    pin = lambda o: pltpu.with_memory_space_constraint(o, pltpu.HBM)
    half = pltpu.VMEM((n, 512, BLK), BF)
    outs = [half, half, pltpu.VMEM((n, 512, 256), BF)]
    scratch = [
        pltpu.VMEM((n // group, 512, 256 * group), BF),
        pltpu.VMEM((2, 512, 256 * group), F32),
        pltpu.SemaphoreType.DMA((n, 2, 2)),
    ]
    if part == 0:
        outs += [pltpu.VMEM((512, 512), BF)] + [pltpu.VMEM((READY, 512, 256), BF)] * 2
        scratch = [
            pltpu.VMEM((512, 512), BF),
            *scratch,
            pltpu.SemaphoreType.DMA((READY, 2, 2)),
            pltpu.SemaphoreType.DMA,
        ]
    return pl.pallas_call(
        functools.partial(grad_kernel, part=part),
        in_specs=[in_smem, in_hbm if part == 0 else near, in_hbm, in_hbm] + [near] * len(ahead),
        out_specs=[near] * len(outs),
        out_shape=outs,
        scratch_shapes=scratch,
        compiler_params=pltpu.CompilerParams(vmem_limit_bytes=24 * MIB),
        cost_estimate=pl.CostEstimate(
            flops=10**6, bytes_accessed=10**4, transcendentals=0
        ),
    )(pos, pin(kc) if part == 0 else kc, pin(acts), pin(err), *ahead)


def store_kernel(pos, *refs):
    blocks, (newerr, sem) = refs[: len(PARTS)], refs[len(PARTS) :]
    copies = []
    for part in range(len(PARTS)):
        for i, item in enumerate(columns_of(pos, part)):
            for k, col, half in windows(item):
                copies.append(
                    pltpu.make_async_copy(
                        blocks[part].at[i, :, half], newerr.at[:, col], sem.at[part, i, k]
                    )
                )
    for copy in copies:
        copy.start()
    for copy in copies:
        copy.wait()


def store_residual(pos, blocks):
    near = pl.BlockSpec(memory_space=pltpu.VMEM)
    return pl.pallas_call(
        store_kernel,
        in_specs=[pl.BlockSpec(memory_space=pltpu.SMEM)] + [near] * len(PARTS),
        out_specs=pl.BlockSpec(memory_space=pl.ANY),
        out_shape=pltpu.HBM((512, 4096), BF),
        scratch_shapes=[pltpu.SemaphoreType.DMA((len(PARTS), max(map(len, PARTS)), 2))],
        compiler_params=pltpu.CompilerParams(vmem_limit_bytes=24 * MIB),
        cost_estimate=pl.CostEstimate(flops=0, bytes_accessed=8 * MIB, transcendentals=0),
    )(pos, *blocks)


def add(*terms):
    total = terms[0].astype(F32)
    for term in terms[1:]:
        total = total + term.astype(F32)
    return total


def y_step(x, which):
    return lax.ppermute(x, ("y", "core"), ring_pairs(which, (4, 2), 0, 1))


def z_step(x, which):
    pairs = []
    for s, d in ring_pairs(which, (4, 2), 0, 1):
        for y in range(4):
            pairs.append(((s // 2 * 4 + y) * 2 + s % 2, (d // 2 * 4 + y) * 2 + d % 2))
    return lax.ppermute(x, ("zh", "y", "core"), pairs)


def swap(x, axis):
    return lax.ppermute(x, axis, [(0, 1), (1, 0)])


def body(acts, key_cotangent, error_rows, error_cols):
    pos = jnp.stack([lax.axis_index(a) for a in ("zh", "y", "core")]).astype(jnp.int32)
    err = error_rows[0, 0]
    parts = [slice(r, r + 512 // CHUNKS) for r in range(0, 512, 512 // CHUNKS)]
    tie = lax.optimization_barrier
    send, keep, err_0, kct, *loaded = grad_part(pos, key_cotangent, acts, err, 0)
    ahead = add(keep, swap(send, "core")).astype(BF)
    pos, ahead = tie((pos, ahead))
    got_0 = y_step(ahead, 0)
    send, keep, err_1 = grad_part(pos, kct, acts, err, 1, loaded)
    near = [swap(send[k : k + 2], "core") for k in range(0, 8, 2)]
    one, two = jnp.concatenate(near[: 2]), near[2 :]
    ahead = add(keep[:4], one).astype(BF)
    _, two = tie((ahead, two))
    got_1 = y_step(ahead, 0)
    ahead = add(keep[4:], jnp.concatenate(two), got_0).astype(BF)
    pos, ahead = tie((pos, ahead))
    got_2 = y_step(ahead, 1)
    send, keep, err_2 = grad_part(pos, kct, acts, err, 2)
    got = tie(add(got_1, got_2))
    swapped = swap(send, "core")
    mine = [add(keep[:, p], swapped[:, p], got[:, p]) for p in parts]
    pos, *mine = tie((pos, *mine))
    newerr = store_residual(pos, (err_0, err_1, err_2))
    got = [z_step(m[2:].astype(BF), 0) for m in mine]
    mine = [add(m[:2], g) for m, g in zip(mine, got)]
    got = [z_step(m[1].astype(BF), 1) for m in mine]
    summed = jnp.concatenate([add(m[0], g) for m, g in zip(mine, got)])

    carried_two = summed * (1.0 / 32.0) + error_cols[0]
    sent_two = lax.optimization_barrier(squash(carried_two))
    new_cols = carried_two - sent_two.astype(F32)
    swapped = swap(sent_two, "zl")
    sent_two, new_cols = tie((sent_two, new_cols))
    total = add(sent_two, swapped)
    near = [
        lax.ppermute(total.astype(BF), "x", [(i, (i + d) % 4) for i in range(4)]) for d in (1, 3, 2)
    ]
    averaged = (add(total, *near) * 0.125).astype(BF)
    return averaged, newerr[None, None], new_cols[None]


def solution(mesh):
    fine = Mesh(mesh.devices.reshape(4, 4, 2, 2, 4), ("zh", "y", "core", "zl", "x"))
    row, col = ("zh", "y", "core"), ("zl", "x")
    in_specs = (
        P(row + col, None),
        P(row + col, None),
        P(row, col, None, None),
        P(col, None, row),
    )
    out_specs = (P(None, row), P(row, col, None, None), P(col, None, row))
    return jax.shard_map(body, mesh=fine, in_specs=in_specs, out_specs=out_specs, check_vma=False)
```

```python
import functools

import jax
import jax.numpy as jnp
from jax import lax
from jax.experimental import pallas as pl
from jax.experimental.pallas import tpu as pltpu
from jax.sharding import Mesh
from jax.sharding import PartitionSpec as P

BLK = 128
BF = jnp.bfloat16
F32 = jnp.float32
MIB = 2**20
CHUNKS = 2
DEPTH = 4
GROUP = (2, 2, 1)
READY = 4
PARTS = (
    tuple(("far", i) for i in range(4)),
    tuple(("one", i) for i in range(4)) + tuple(("two", i) for i in range(4)),
    tuple(("own", i) for i in range(4)),
)
SEND_SLOT = ((0, 2, 1, 3), (0, 2, 1, 3, 4, 6, 5, 7), (0, 2, 1, 3))


def partner(which, i, core):
    flip = lax.bitwise_xor(i, 1)
    turn = 3 - i
    return jnp.where(core == which, flip, turn)


def ring_pairs(which, shape, ring, core):
    def linear(pos):
        out = 0
        for p, n in zip(pos, shape):
            out = out * n + p
        return out

    pairs = []
    for r in range(4):
        for c in range(2):
            src, dst = [0, 0], [0, 0]
            src[ring], src[core] = r, c
            dst[ring], dst[core] = (r ^ 1 if c == which else 3 - r), c
            pairs.append((linear(src), linear(dst)))
    return pairs


def squash(v):
    m = jnp.sum(jnp.abs(v), axis=1, keepdims=True) * (1.0 / BLK) + 1e-6
    return (m * jnp.tanh(v * (1.0 / m))).astype(BF)


def items_of(pos, kind):
    zh, y, core = pos[0], pos[1], pos[2]
    other = 1 - core
    zs = (zh, partner(1, zh, core), partner(0, zh, core), lax.bitwise_xor(zh, 2))
    y1, y2 = partner(0, y, core), partner(1, y, core)
    if kind in ("far", "own"):
        whole = y if kind == "own" else lax.bitwise_xor(y, 2)
        return [[(z * 4 + whole) * 256] for z in zs]
    left, right = (y1, y2) if kind == "one" else (y2, y1)
    return [[((z * 4 + left) * 2 + core) * BLK, ((z * 4 + right) * 2 + other) * BLK] for z in zs]


def columns_of(pos, part):
    kinds = {kind: items_of(pos, kind) for kind, _ in PARTS[part]}
    return [kinds[kind][i] for kind, i in PARTS[part]]


def windows(starts, offset=0):
    width = 256 // len(starts)
    for k, start in enumerate(starts):
        yield k, pl.ds(pl.multiple_of(start, width), width), pl.ds(offset + k * width, width)


def grad_kernel(pos, kc, acts, err, *refs, part):
    if part == 0:
        send, keep, ev, kct, ready_a, ready_e, kcv, av, gv, asem, rsem, ksem = refs
    elif part == 1:
        ready_a, ready_e, send, keep, ev, av, gv, asem = refs
        kct = kc
    else:
        send, keep, ev, av, gv, asem = refs
        kct = kc
    core = pos[2]
    items = columns_of(pos, part)
    n, group = len(items), GROUP[part]
    first = READY if part == 1 else 0

    def loads(i):
        for k, col, half in windows(items[i], 256 * (i % group)):
            yield pltpu.make_async_copy(acts.at[:, col], av.at[i // group, :, half], asem.at[i, k, 0])
        for k, col, half in windows(items[i]):
            yield pltpu.make_async_copy(err.at[:, col], ev.at[i, :, half], asem.at[i, k, 1])

    def loads_ahead():
        for i, item in enumerate(columns_of(pos, 1)[:READY]):
            for k, col, half in windows(item, 256 * (i % 2)):
                yield pltpu.make_async_copy(acts.at[:, col], ready_a.at[i // 2, :, half], rsem.at[i, k, 0])
            for k, col, half in windows(item):
                yield pltpu.make_async_copy(err.at[:, col], ready_e.at[i, :, half], rsem.at[i, k, 1])

    def ready(p):
        for i in range(p * group, (p + 1) * group):
            if i >= first:
                for copy in loads(i):
                    copy.wait()

    def source(p):
        return ready_a[p] if p * group < first else av[p]

    if part == 0:
        load_kc = pltpu.make_async_copy(kc, kcv, ksem)
        load_kc.start()
    for i in range(first, first + DEPTH):
        for copy in loads(i):
            copy.start()
    if part == 0:
        load_kc.wait()
        kct[...] = kcv[...].T
    ready(0)
    if part == 0:
        for copy in loads_ahead():
            copy.start()
    gv[0] = jnp.dot(kct[...], source(0), preferred_element_type=F32)
    for p in range(n // group):
        members = range(p * group, (p + 1) * group)
        for i in members:
            if i >= first and i + DEPTH < n:
                for copy in loads(i + DEPTH):
                    copy.start()
        more = p + 1 < n // group
        if more:
            ready(p + 1)
        for r in range(0, 512, 256):
            rows = slice(r, r + 256)
            if more:
                gv[(p + 1) % 2, rows] = jnp.dot(kct[rows], source(p + 1), preferred_element_type=F32)
            for i in members:
                q = []
                for k in range(2):
                    s = slice(k * BLK, (k + 1) * BLK)
                    t = 256 * (i % group) + k * BLK
                    residual = (ready_e if i < first else ev)[i, rows, s]
                    v = gv[p % 2, rows, t : t + BLK] + residual.astype(F32)
                    q.append(squash(v))
                    ev[i, rows, s] = (v - q[k].astype(F32)).astype(BF)
                if len(items[i]) == 1:
                    q = [jnp.where(core == 0, q[0], q[1]), jnp.where(core == 0, q[1], q[0])]
                keep[i, rows] = q[0]
                send[SEND_SLOT[part][i], rows] = q[1]
    if part == 0:
        for copy in loads_ahead():
            copy.wait()


def grad_part(pos, kc, acts, err, part, ahead=()):
    n, group = len(PARTS[part]), GROUP[part]
    in_hbm = pl.BlockSpec(memory_space=pl.ANY)
    near = pl.BlockSpec(memory_space=pltpu.VMEM)
    in_smem = pl.BlockSpec(memory_space=pltpu.SMEM)
    pin = lambda o: pltpu.with_memory_space_constraint(o, pltpu.HBM)
    half = pltpu.VMEM((n, 512, BLK), BF)
    outs = [half, half, pltpu.VMEM((n, 512, 256), BF)]
    scratch = [
        pltpu.VMEM((n // group, 512, 256 * group), BF),
        pltpu.VMEM((2, 512, 256 * group), F32),
        pltpu.SemaphoreType.DMA((n, 2, 2)),
    ]
    if part == 0:
        outs += [pltpu.VMEM((512, 512), BF)] + [pltpu.VMEM((READY // 2, 512, 512), BF), pltpu.VMEM((READY, 512, 256), BF)]
        scratch = [
            pltpu.VMEM((512, 512), BF),
            *scratch,
            pltpu.SemaphoreType.DMA((READY, 2, 2)),
            pltpu.SemaphoreType.DMA,
        ]
    return pl.pallas_call(
        functools.partial(grad_kernel, part=part),
        in_specs=[in_smem, in_hbm if part == 0 else near, in_hbm, in_hbm] + [near] * len(ahead),
        out_specs=[near] * len(outs),
        out_shape=outs,
        scratch_shapes=scratch,
        compiler_params=pltpu.CompilerParams(vmem_limit_bytes=24 * MIB),
        cost_estimate=pl.CostEstimate(
            flops=10**6, bytes_accessed=10**4, transcendentals=0
        ),
    )(pos, pin(kc) if part == 0 else kc, pin(acts), pin(err), *ahead)


def store_kernel(pos, *refs):
    blocks, (newerr, sem) = refs[: len(PARTS)], refs[len(PARTS) :]
    copies = []
    for part in range(len(PARTS)):
        for i, item in enumerate(columns_of(pos, part)):
            for k, col, half in windows(item):
                copies.append(
                    pltpu.make_async_copy(
                        blocks[part].at[i, :, half], newerr.at[:, col], sem.at[part, i, k]
                    )
                )
    for copy in copies:
        copy.start()
    for copy in copies:
        copy.wait()


def store_residual(pos, blocks):
    near = pl.BlockSpec(memory_space=pltpu.VMEM)
    return pl.pallas_call(
        store_kernel,
        in_specs=[pl.BlockSpec(memory_space=pltpu.SMEM)] + [near] * len(PARTS),
        out_specs=pl.BlockSpec(memory_space=pl.ANY),
        out_shape=pltpu.HBM((512, 4096), BF),
        scratch_shapes=[pltpu.SemaphoreType.DMA((len(PARTS), max(map(len, PARTS)), 2))],
        compiler_params=pltpu.CompilerParams(vmem_limit_bytes=24 * MIB),
        cost_estimate=pl.CostEstimate(flops=0, bytes_accessed=8 * MIB, transcendentals=0),
    )(pos, *blocks)


def add(*terms):
    total = terms[0].astype(F32)
    for term in terms[1:]:
        total = total + term.astype(F32)
    return total


def y_step(x, which):
    return lax.ppermute(x, ("y", "core"), ring_pairs(which, (4, 2), 0, 1))


def z_step(x, which):
    pairs = []
    for s, d in ring_pairs(which, (4, 2), 0, 1):
        for y in range(4):
            pairs.append(((s // 2 * 4 + y) * 2 + s % 2, (d // 2 * 4 + y) * 2 + d % 2))
    return lax.ppermute(x, ("zh", "y", "core"), pairs)


def swap(x, axis):
    return lax.ppermute(x, axis, [(0, 1), (1, 0)])


def body(acts, key_cotangent, error_rows, error_cols):
    pos = jnp.stack([lax.axis_index(a) for a in ("zh", "y", "core")]).astype(jnp.int32)
    err = error_rows[0, 0]
    parts = [slice(r, r + 512 // CHUNKS) for r in range(0, 512, 512 // CHUNKS)]
    tie = lax.optimization_barrier
    send, keep, err_0, kct, *loaded = grad_part(pos, key_cotangent, acts, err, 0)
    ahead = add(keep, swap(send, "core")).astype(BF)
    pos, ahead = tie((pos, ahead))
    got_0 = y_step(ahead, 0)
    send, keep, err_1 = grad_part(pos, kct, acts, err, 1, loaded)
    near = [swap(send[k : k + 2], "core") for k in range(0, 8, 2)]
    one, two = jnp.concatenate(near[: 2]), near[2 :]
    ahead = add(keep[:4], one).astype(BF)
    _, two = tie((ahead, two))
    got_1 = y_step(ahead, 0)
    ahead = add(keep[4:], jnp.concatenate(two), got_0).astype(BF)
    pos, ahead = tie((pos, ahead))
    got_2 = y_step(ahead, 1)
    send, keep, err_2 = grad_part(pos, kct, acts, err, 2)
    got = tie(add(got_1, got_2))
    swapped = swap(send, "core")
    mine = [add(keep[:, p], swapped[:, p], got[:, p]) for p in parts]
    pos, *mine = tie((pos, *mine))
    newerr = store_residual(pos, (err_0, err_1, err_2))
    got = [z_step(m[2:].astype(BF), 0) for m in mine]
    mine = [add(m[:2], g) for m, g in zip(mine, got)]
    got = [z_step(m[1].astype(BF), 1) for m in mine]
    summed = jnp.concatenate([add(m[0], g) for m, g in zip(mine, got)])

    carried_two = summed * (1.0 / 32.0) + error_cols[0]
    sent_two = lax.optimization_barrier(squash(carried_two))
    new_cols = carried_two - sent_two.astype(F32)
    swapped = swap(sent_two, "zl")
    sent_two, new_cols = tie((sent_two, new_cols))
    total = add(sent_two, swapped)
    near = [
        lax.ppermute(total.astype(BF), "x", [(i, (i + d) % 4) for i in range(4)]) for d in (1, 3, 2)
    ]
    averaged = (add(total, *near) * 0.125).astype(BF)
    return averaged, newerr[None, None], new_cols[None]


def solution(mesh):
    fine = Mesh(mesh.devices.reshape(4, 4, 2, 2, 4), ("zh", "y", "core", "zl", "x"))
    row, col = ("zh", "y", "core"), ("zl", "x")
    in_specs = (
        P(row + col, None),
        P(row + col, None),
        P(row, col, None, None),
        P(col, None, row),
    )
    out_specs = (P(None, row), P(row, col, None, None), P(col, None, row))
    return jax.shard_map(body, mesh=fine, in_specs=in_specs, out_specs=out_specs, check_vma=False)
```
